32 devices in a mesh: gx: 8 (over z, y), gy: 4 (over x, core).
Axes of the slice: x: 2, y: 2, z: 4, core: 2. Of those that a mesh axis runs over, the one named last changes fastest.
Arguments:
- fields: float32 [5, 4, 256, 512], P(None, None, 'gx', 'gy'), may hold values from -6 to 6
- viscosity: float32 [4, 256, 512], P(None, 'gx', 'gy'), may hold values from 0.03 to 0.3
- precursor: float32 [5, 4, 512], P(None, None, 'gy'), may hold values from -6 to 6
- tile_index: int32 [512], P('gy'), may hold values from 0 to 511, as said below
- fine_fields: float32 [512, 5, 4, 4, 256], P(('gx', 'gy')), may hold values from -6 to 6
- fine_viscosity: float32 [512, 4, 4, 256], P(('gx', 'gy')), may hold values from 0.03 to 0.3
- partner_gx: int32 [512], P(('gx', 'gy')), may hold values from 0 to 7, as said below
- partner_col: int32 [512], P(('gx', 'gy')), may hold values from 0 to 31
Outputs:
- fields_out: float32 [5, 4, 256, 512], P(None, None, 'gx', 'gy')
- fine_out: float32 [512, 5, 4, 4, 256], P(('gx', 'gy'))
The draws below stay inside these ranges and needn't reach their ends.
Inputs may be any that keep to these rules, and one draw needn't show every extreme that they name: `tile_index`: inlet cell y takes precursor cell (y + s) mod 512, where s is drawn for each aligned block of 128 cells. `partner_gx`: each device's tiles are glued to outer devices of its own gy row: exactly 2 tiles to each of 8 distinct gx indices; in every gy row one gx index receives 2 tiles from every device of the row.
All inputs are finite; a program needn't handle non-finite values.
Results may differ from the reference program's by a relative error of at most 0.00005.
Values sent between devices are 32-bit elements; how exact they have to be, the bound alone decides.
A program may use at most 64 MiB of HBM per device.

```python
import math
import jax
import jax.numpy as jnp
from jax import lax

F = 5
Z = 4
CX = 32
CY = 128
RX = 4
PW = 512
CAP = 2
RT_DEV = 16
NR = 512
NX = 256
NY = 512
RW = 256
N_GX = 8
N_GY = 4


def draw_tile_index(key, part):
    shifts = jax.random.randint(jax.random.fold_in(key, 11), (NY // CY,), 0, PW)
    positions = jnp.arange(NY, dtype=jnp.int32)
    return ((positions + shifts[positions // CY]) % PW).astype(jnp.int32)


def draw_partner_gx(key, part):
    hot_target = jax.random.randint(jax.random.fold_in(key, 21), (N_GY,), 0, N_GX)
    shift_draw = jax.random.randint(jax.random.fold_in(key, 22), (N_GX, N_GY), 0, N_GX - 1)
    group_of = jnp.arange(RT_DEV, dtype=jnp.int32) // CAP
    other_target = (hot_target[None, :, None] + 1 + (group_of[None, None, :] - 1 + shift_draw[:, :, None]) % (N_GX - 1)) % N_GX
    targets = jnp.where(group_of[None, None, :] == 0, hot_target[None, :, None], other_target)
    targets = targets.reshape(N_GX * N_GY, RT_DEV)
    device_keys = jax.random.split(jax.random.fold_in(key, 23), N_GX * N_GY)
    shuffles = jax.vmap(lambda subkey: jax.random.permutation(subkey, RT_DEV))(device_keys)
    mixed = jnp.take_along_axis(targets, shuffles, axis=1)
    return mixed.reshape(NR).astype(jnp.int32)


def place_ends(array, key, least, high):
    shape = array.shape
    index_at = [jax.random.randint(jax.random.fold_in(key, axis), (), 0, shape[axis]) for axis in range(len(shape))]
    array = array.at[tuple(index_at)].set(least)
    longest = shape.index(max(shape))
    index_at[longest] = (index_at[longest] + 1) % shape[longest]
    return array.at[tuple(index_at)].set(high)


def steps_of(stream_key, shape, shards, smallest, top_value):
    loudness, own = 1.0, jax.random.fold_in(stream_key, 6)
    for axis_at, parts in shards:
        heights = jnp.exp(jax.random.uniform(jax.random.fold_in(own, axis_at), (parts,), jnp.float32, smallest / len(shards), top_value / len(shards)))
        loudness = loudness * jnp.repeat(heights, shape[axis_at] // parts).reshape([-1 if axis == axis_at else 1 for axis in range(len(shape))])
    return loudness


def noise(own_key, shape, scale, reach, pieces=(), kind=jnp.bfloat16):
    values = scale * jax.random.normal(own_key, shape, jnp.float32)
    if pieces:
        values = values * steps_of(own_key, shape, pieces, -0.22, 0.18)
    return jnp.clip(values, -reach, reach).astype(kind)


def setup_inputs(seed: int = 0) -> dict:
    arg_keys = jax.random.split(jax.random.key(seed), 9)
    fields = noise(arg_keys[0], (F, Z, NX, NY), 1.0, 6.0, ((2, 8), (3, 4)), jnp.float32)
    viscosity = jnp.clip(jnp.exp(math.log(0.3) - 2.3025852 * jax.random.uniform(arg_keys[1], (Z, NX, NY), jnp.float32) ** steps_of(arg_keys[1], (Z, NX, NY), ((1, 8), (2, 4)), -0.2, 0.2)), 0.03, 0.3)
    precursor = noise(arg_keys[2], (F, Z, PW), 1.0, 6.0, ((2, 4),), jnp.float32)
    tile_index = draw_tile_index(jax.random.fold_in(arg_keys[8], 71), 0)
    fine_fields = noise(arg_keys[4], (NR, F, Z, RX, RW), 1.0, 6.0, ((0, 32),), jnp.float32)
    fine_viscosity = jnp.clip(jnp.exp(math.log(0.3) - 2.3025852 * jax.random.uniform(arg_keys[5], (NR, Z, RX, RW), jnp.float32) ** steps_of(arg_keys[5], (NR, Z, RX, RW), ((0, 32),), -0.2, 0.2)), 0.03, 0.3)
    partner_gx = draw_partner_gx(jax.random.fold_in(arg_keys[8], 71), 0)
    partner_col = place_ends(jax.random.randint(arg_keys[7], (NR,), 0, CX), jax.random.fold_in(arg_keys[7], 1), 0, CX - 1).astype(jnp.int32)
    return dict(fields=fields, viscosity=viscosity, precursor=precursor, tile_index=tile_index, fine_fields=fine_fields, fine_viscosity=fine_viscosity, partner_gx=partner_gx, partner_col=partner_col)


time_step = 0.2
vertical_mix = 0.1
coarse_penalty = 0.5
fine_penalty = 1.0


def tendency(padded, spacing):
    nfield = padded.shape[-4] - 1
    state_part = padded[..., :nfield, :, :, :]
    visc_part = padded[..., nfield:, :, :, :]
    centre = state_part[..., 1:-1, 1:-1]
    q_east = state_part[..., 2:, 1:-1]
    q_west = state_part[..., :-2, 1:-1]
    q_north = state_part[..., 1:-1, 2:]
    q_south = state_part[..., 1:-1, :-2]
    u_flow = centre[..., 0:1, :, :, :]
    v_flow = centre[..., 1:2, :, :, :]
    nu_mid = visc_part[..., 1:-1, 1:-1]
    nu_east = 0.5 * (nu_mid + visc_part[..., 2:, 1:-1])
    nu_west = 0.5 * (nu_mid + visc_part[..., :-2, 1:-1])
    nu_north = 0.5 * (nu_mid + visc_part[..., 1:-1, 2:])
    nu_south = 0.5 * (nu_mid + visc_part[..., 1:-1, :-2])
    advect = (u_flow * (q_east - q_west) + v_flow * (q_north - q_south)) / (2.0 * spacing)
    diffuse = (nu_east * (q_east - centre) - nu_west * (centre - q_west)
               + nu_north * (q_north - centre) - nu_south * (centre - q_south)) / (spacing * spacing)
    q_above = jnp.concatenate([centre[..., 1:, :, :], centre[..., -1:, :, :]], axis=-3)
    q_below = jnp.concatenate([centre[..., :1, :, :], centre[..., :-1, :, :]], axis=-3)
    return diffuse - advect + vertical_mix * (q_above - 2.0 * centre + q_below)


def coarsen(trace_in):
    even_cells = trace_in[..., 0::2]
    odd_cells = trace_in[..., 1::2]
    left_cells = jnp.concatenate([trace_in[..., :1], odd_cells[..., :-1]], axis=-1)
    return 0.25 * left_cells + 0.5 * even_cells + 0.25 * odd_cells


def refine(trace_in):
    shifted = jnp.concatenate([trace_in[..., 1:], trace_in[..., -1:]], axis=-1)
    odd_cells = 0.5 * (trace_in + shifted)
    joined = jnp.stack([trace_in, odd_cells], axis=-1)
    return joined.reshape(trace_in.shape[:-1] + (2 * trace_in.shape[-1],))


def reference(fields, viscosity, precursor, tile_index, fine_fields, fine_viscosity, partner_gx, partner_col):
    inflow = precursor[:, :, tile_index]
    stacked = jnp.concatenate([fields, viscosity[None]], axis=0)
    inlet_ghost = jnp.concatenate([inflow, viscosity[None, :, 0, :]], axis=0)
    xpadded = jnp.concatenate([inlet_ghost[:, :, None, :], stacked, stacked[:, :, -1:, :]], axis=2)
    padded = jnp.concatenate([xpadded[..., -1:], xpadded, xpadded[..., :1]], axis=3)
    coarse_rate = tendency(padded, 1.0)

    fine_stack = jnp.concatenate([fine_fields, fine_viscosity[:, None]], axis=1)
    blocks = fine_stack.reshape((N_GX * N_GY, RT_DEV) + fine_stack.shape[1:])

    def block_rate(one_block):
        widened = jnp.pad(one_block, ((0, 0), (0, 0), (0, 0), (1, 1), (1, 1)), mode="edge")
        return tendency(widened, 0.5)

    fine_rate = lax.map(block_rate, blocks).reshape(fine_fields.shape)

    tile_ids = jnp.arange(NR, dtype=jnp.int32)
    row_of = (tile_ids // RT_DEV) % N_GY
    column = (partner_gx * CX + partner_col).astype(jnp.int32)
    span_cells = (row_of[:, None] * CY + jnp.arange(CY, dtype=jnp.int32)[None, :]).astype(jnp.int32)
    coarse_trace = jnp.transpose(fields[:, :, column[:, None], span_cells], (2, 0, 1, 3))
    fine_trace = fine_fields[:, :, :, 0, :]
    mismatch = coarse_penalty * (coarsen(fine_trace) - coarse_trace)
    coarse_sat = jnp.zeros_like(fields).at[:, :, column[:, None], span_cells].add(jnp.transpose(mismatch, (1, 2, 0, 3)))
    fields_out = fields + time_step * (coarse_rate + coarse_sat)
    fine_sat = fine_penalty * (refine(coarse_trace) - fine_trace)
    total_rate = fine_rate.at[:, :, :, 0, :].add(fine_sat)
    fine_out = fine_fields + time_step * total_rate
    return fields_out, fine_out
```

```python
import functools

import jax
import jax.numpy as jnp
from jax import lax
from jax.experimental import pallas as pl
from jax.experimental.pallas import tpu as pltpu
from jax.sharding import PartitionSpec as P

CAP = 2
LANES = 128

time_step = 0.2
vertical_mix = 0.1
coarse_penalty = 0.5
fine_penalty = 1.0


def lane_take(rows, index):
    return jnp.take_along_axis(rows, index, axis=1, mode="promise_in_bounds")


def kernel(
    ngx, ngy, nfield, levels, columns, tiles, width,
    f_ref, n_ref, p_ref, ti_ref, g_ref, gn_ref, pgx_ref, pcol_ref,
    fo_ref, go_ref,
    tid, col_send, col_recv, ctr, tr_send, tr_recv, an_send, an_recv,
    hx_send, hx_recv, hy_send, hy_recv, pr,
    col_ss, col_rs, tr_ss, tr_rs, an_ss, an_rs, hx_ss, hx_rs, hy_ss, hy_rs, pr_ss, pr_rs,
):
    mx, my = lax.axis_index("gx"), lax.axis_index("gy")
    nz = nfield * levels

    def x_peer(d):
        return (lax.rem(mx + d + ngx, ngx), my)

    def y_peer(d):
        return (mx, lax.rem(my + d + ngy, ngy))

    barrier = pltpu.get_barrier_semaphore()
    for d in range(1, ngx):
        pl.semaphore_signal(barrier, inc=1, device_id=x_peer(d), device_id_type=pl.DeviceIdType.MESH)
    for d in range(1, ngy):
        pl.semaphore_signal(barrier, inc=1, device_id=y_peer(d), device_id_type=pl.DeviceIdType.MESH)

    for d in range(ngx):
        goal = lax.rem(mx + d, ngx)
        first, last = jnp.int32(tiles), jnp.int32(-1)
        for t in range(tiles):
            hit = pgx_ref[t] == goal
            last = jnp.where(hit, t, last)
            u = tiles - 1 - t
            first = jnp.where(pgx_ref[u] == goal, u, first)
        for c, at in enumerate((first, last)):
            inside = jnp.clip(at, 0, tiles - 1)
            tid[d, c] = inside
            value = jnp.where(last < 0, -1, pcol_ref[inside])
            col_send[d, c] = value
            if d == 0:
                col_recv[d, c] = value

    rows = lax.broadcasted_iota(jnp.int32, (columns, LANES), 0)
    lanes = lax.broadcasted_iota(jnp.int32, (columns, LANES), 1)
    lane_z = lax.broadcasted_iota(jnp.int32, (nz, LANES), 1)

    def slab(k):
        return f_ref[k * columns : (k + 1) * columns, :]

    def nslab(z):
        return n_ref[z * columns : (z + 1) * columns, :]

    for side, row in ((0, columns - 1), (1, 0)):
        hx_send[side, 0:nz, :] = f_ref[pl.ds(row, nz, stride=columns), :]
        hx_send[side, nz : nz + levels, :] = n_ref[pl.ds(row, levels, stride=columns), :]
    for side, lane in ((0, LANES - 1), (1, 0)):
        packed = jnp.zeros((columns, LANES), jnp.float32)
        for k in range(nz + levels):
            s = slab(k) if k < nz else nslab(k - nz)
            packed = jnp.where(
                lanes == k, jnp.broadcast_to(s[:, lane : lane + 1], (columns, LANES)), packed
            )
        hy_send[side] = packed
    for f in range(nfield):
        pr[0, f * levels : (f + 1) * levels, :] = p_ref[f]

    pl.semaphore_wait(barrier, ngx + ngy - 2)

    def remote(src, dst, ss, rs, to):
        return pltpu.make_async_remote_copy(
            src_ref=src, dst_ref=dst, send_sem=ss, recv_sem=rs,
            device_id=to, device_id_type=pl.DeviceIdType.MESH,
        )

    col = [remote(col_send.at[d], col_recv.at[d], col_ss.at[d], col_rs.at[d], x_peer(d)) for d in range(1, ngx)]
    for c in col:
        c.start()
    halo = [
        remote(hx_send.at[0], hx_recv.at[0], hx_ss.at[0], hx_rs.at[0], x_peer(1)),
        remote(hx_send.at[1], hx_recv.at[1], hx_ss.at[1], hx_rs.at[1], x_peer(-1)),
        remote(hy_send.at[0], hy_recv.at[0], hy_ss.at[0], hy_rs.at[0], y_peer(1)),
        remote(hy_send.at[1], hy_recv.at[1], hy_ss.at[1], hy_rs.at[1], y_peer(-1)),
    ]
    for c in halo:
        c.start()
    plane = [remote(pr.at[0], pr.at[d], pr_ss.at[d], pr_rs.at[d], y_peer(d)) for d in range(1, ngy)]

    @pl.when(mx == 0)
    def _():
        for c in plane:
            c.start()

    even = (2 * lane_z) % LANES

    def coarsen(t, carry):
        g0 = g_ref[t, pl.ds(0, nz, stride=8), :]
        g1 = g_ref[t, pl.ds(4, nz, stride=8), :]
        r0, r1 = pltpu.roll(g0, 1, 1), pltpu.roll(g1, 1, 1)
        l0 = jnp.where(lane_z == 0, g0, r0)
        l1 = jnp.where(lane_z == 0, r0, r1)
        y0 = 0.5 * g0 + 0.25 * (l0 + pltpu.roll(g0, LANES - 1, 1))
        y1 = 0.5 * g1 + 0.25 * (l1 + pltpu.roll(g1, LANES - 1, 1))
        ctr[t] = jnp.where(lane_z < LANES // 2, lane_take(y0, even), lane_take(y1, even))
        return carry

    lax.fori_loop(0, tiles, coarsen, 0)
    traces = [remote(tr_send.at[d], tr_recv.at[d], tr_ss.at[d], tr_rs.at[d], x_peer(d)) for d in range(1, ngx)]
    for d in range(ngx):
        for c in range(CAP):
            if d == 0:
                tr_recv[0, c] = ctr[tid[0, c]]
            else:
                tr_send[d, c] = ctr[tid[d, c]]
        if d:
            traces[d - 1].start()

    answers = [remote(an_send.at[d], an_recv.at[d], an_ss.at[d], an_rs.at[d], x_peer(-d)) for d in range(1, ngx)]
    for d in range(ngx):
        if d:
            col[d - 1].wait_recv()
        for c in range(CAP):
            at = jnp.maximum(col_recv[d, c], 0)
            for k in range(nz):
                row = f_ref[pl.ds(k * columns + at, 1), :]
                if d:
                    an_send[d, c, k : k + 1, :] = row
                else:
                    an_recv[0, c, k : k + 1, :] = row
        if d:
            answers[d - 1].start()

    row8 = lax.broadcasted_iota(jnp.int32, (8, LANES), 0)
    lane8 = lax.broadcasted_iota(jnp.int32, (8, LANES), 1)
    x_last = (row8 % 4) == 3
    is_glue = (row8 % 4) == 0
    y_last = (lane8 == LANES - 1) & (row8 >= 4)
    lane_last, lane_first = lane8 == LANES - 1, lane8 == 0
    zero = jnp.zeros((8, LANES), jnp.float32)
    own = jnp.where(is_glue, 1.0 - time_step * fine_penalty, 1.0)

    def up_x(q):
        return pltpu.roll(q, 7, 0)

    def down_x(q):
        return pltpu.roll(q, 1, 0)

    def up_y(q):
        r = pltpu.roll(q, LANES - 1, 1)
        return jnp.where(lane_last, pltpu.roll(r, 4, 0), r)

    def down_y(q):
        r = pltpu.roll(q, 1, 1)
        return jnp.where(lane_first, pltpu.roll(r, 4, 0), r)

    def fine(t, carry):
        for z in range(levels):
            n = gn_ref[t, z * 8 : z * 8 + 8, :]
            u = time_step * g_ref[t, z * 8 : z * 8 + 8, :]
            v = time_step * g_ref[t, (levels + z) * 8 : (levels + z) * 8 + 8, :]
            n = (2.0 * time_step) * n
            nx = n + up_x(n)
            ny = n + up_y(n)
            ae, aw = nx - u, down_x(nx) + u
            an, as_ = ny - v, down_y(ny) + v
            for f in range(nfield):
                k = f * levels + z
                q = g_ref[t, k * 8 : k * 8 + 8, :]
                e = jnp.where(x_last, zero, up_x(q) - q)
                w = down_x(e)
                nn = jnp.where(y_last, zero, up_y(q) - q)
                s = down_y(nn)
                out = own * q + ae * e - aw * w + an * nn - as_ * s
                if z < levels - 1:
                    out = out + (time_step * vertical_mix) * (g_ref[t, (k + 1) * 8 : (k + 1) * 8 + 8, :] - q)
                if z > 0:
                    out = out - (time_step * vertical_mix) * (q - g_ref[t, (k - 1) * 8 : (k - 1) * 8 + 8, :])
                go_ref[t, k * 8 : k * 8 + 8, :] = out
        return carry

    lax.fori_loop(0, tiles, fine, 0)

    for c in halo:
        c.wait_recv()

    @pl.when(mx == 0)
    def _():
        for c in plane:
            c.wait_recv()
        index = jnp.broadcast_to(ti_ref[...], (nz, LANES))
        per = LANES // width
        inflow = jnp.zeros((nz, LANES), jnp.float32)
        for b in range(ngy * width // LANES):
            parts = [pr[lax.rem(my - (b * per + i) + ngy, ngy)] for i in range(per)]
            block = parts[0] if per == 1 else jnp.concatenate(parts, axis=1)
            inflow = jnp.where(index // LANES == b, lane_take(block, index % LANES), inflow)
        hx_recv[0, 0:nz, :] = inflow
        hx_recv[0, nz : nz + levels, :] = n_ref[pl.ds(0, levels, stride=columns), :]

    @pl.when(mx == ngx - 1)
    def _():
        hx_recv[1, 0:nz, :] = f_ref[pl.ds(columns - 1, nz, stride=columns), :]
        hx_recv[1, nz : nz + levels, :] = n_ref[pl.ds(columns - 1, levels, stride=columns), :]

    for c in traces:
        c.wait_recv()
    count = jnp.zeros((columns, LANES), jnp.float32)
    for d in range(ngx):
        for c in range(CAP):
            count = count + jnp.where(rows == col_recv[d, c], 1.0, 0.0)
    keep = 1.0 - (time_step * coarse_penalty) * count

    def glue(k, carry):
        total = jnp.zeros((columns, LANES), jnp.float32)
        for d in range(ngx):
            for c in range(CAP):
                row = tr_recv[d, c, pl.ds(k, 1), :]
                total = total + jnp.where(
                    rows == col_recv[d, c], jnp.broadcast_to(row, (columns, LANES)), 0.0
                )
        at = pl.multiple_of(k * columns, columns)
        fo_ref[pl.ds(at, columns), :] = (
            keep * f_ref[pl.ds(at, columns), :] + (time_step * coarse_penalty) * total
        )
        return carry

    lax.fori_loop(0, nz, glue, 0)

    def around(q, k):
        e = jnp.where(rows == columns - 1, hx_recv[1, k : k + 1, :], pltpu.roll(q, columns - 1, 0))
        w = jnp.where(rows == 0, hx_recv[0, k : k + 1, :], pltpu.roll(q, 1, 0))
        n = jnp.where(lanes == LANES - 1, hy_recv[1, :, k : k + 1], pltpu.roll(q, LANES - 1, 1))
        s = jnp.where(lanes == 0, hy_recv[0, :, k : k + 1], pltpu.roll(q, 1, 1))
        return e, w, n, s

    half = 0.5 * time_step
    for z in range(levels):
        n = nslab(z)
        ne, nw, nn, ns = around(n, nz + z)
        u, v = slab(z), slab(levels + z)
        ae, aw = half * (n + ne - u), half * (n + nw + u)
        an, as_ = half * (n + nn - v), half * (n + ns + v)
        for f in range(nfield):
            k = f * levels + z
            q = slab(k)
            e, w, north, south = around(q, k)
            out = ae * (e - q) - aw * (q - w) + an * (north - q) - as_ * (q - south)
            if z < levels - 1:
                out = out + (time_step * vertical_mix) * (slab(k + 1) - q)
            if z > 0:
                out = out - (time_step * vertical_mix) * (q - slab(k - 1))
            at = k * columns
            fo_ref[at : at + columns, :] = fo_ref[at : at + columns, :] + out

    for c in answers:
        c.wait_recv()
    low = lane_z // 2
    low_up = low + lane_z % 2
    high = low + LANES // 2
    high_up = jnp.minimum(low_up + LANES // 2, LANES - 1)

    def settle(t, carry):
        goal = pgx_ref[t]
        d = lax.rem(goal - mx + ngx, ngx)
        c = jnp.where(tid[d, 0] == t, 0, 1)
        a = (0.5 * time_step * fine_penalty) * an_recv[d, c]
        r0 = lane_take(a, low) + lane_take(a, low_up)
        r1 = lane_take(a, high) + lane_take(a, high_up)
        for k in range(nz):
            b0 = jnp.broadcast_to(r0[k : k + 1, :], (8, LANES))
            b1 = jnp.broadcast_to(r1[k : k + 1, :], (8, LANES))
            add = jnp.where(is_glue, jnp.where(row8 < 4, b0, b1), zero)
            go_ref[t, k * 8 : k * 8 + 8, :] = go_ref[t, k * 8 : k * 8 + 8, :] + add
        return carry

    lax.fori_loop(0, tiles, settle, 0)

    for c in col + halo + traces + answers:
        c.wait_send()

    @pl.when(mx == 0)
    def _():
        for c in plane:
            c.wait_send()


def halves_in(a):
    lead = a.shape[:-2]
    a = a.reshape(lead + (a.shape[-2], 2, LANES))
    a = jnp.swapaxes(a, -3, -2)
    return a.reshape(lead + (2 * a.shape[-2], LANES))


def halves_out(a):
    lead = a.shape[:-2]
    a = a.reshape(lead + (2, a.shape[-2] // 2, LANES))
    a = jnp.swapaxes(a, -3, -2)
    return a.reshape(lead + (a.shape[-3], 2 * LANES))


def on_device(
    fields, viscosity, precursor, tile_index, fine_fields, fine_viscosity, partner_gx, partner_col
):
    ngx, ngy = lax.axis_size("gx"), lax.axis_size("gy")
    nfield, levels, columns, span = fields.shape
    nz = nfield * levels
    tiles = fine_fields.shape[0]
    width = precursor.shape[2]
    f32, i32 = jnp.float32, jnp.int32
    g = halves_in(fine_fields).reshape(tiles, nz * 8, LANES)
    gn = halves_in(fine_viscosity).reshape(tiles, levels * 8, LANES)
    vmem = pl.BlockSpec(memory_space=pltpu.VMEM)
    smem = pl.BlockSpec(memory_space=pltpu.SMEM)
    dma = pltpu.SemaphoreType.DMA
    trace = pltpu.VMEM((ngx, CAP, nz, LANES), f32)
    fo, go = pl.pallas_call(
        functools.partial(kernel, ngx, ngy, nfield, levels, columns, tiles, width),
        out_shape=(
            jax.ShapeDtypeStruct((nz * columns, span), f32),
            jax.ShapeDtypeStruct((tiles, nz * 8, LANES), f32),
        ),
        in_specs=[vmem] * 6 + [smem] * 2,
        out_specs=(vmem, vmem),
        scratch_shapes=[
            pltpu.SMEM((ngx, CAP), i32),
            pltpu.SMEM((ngx, LANES), i32),
            pltpu.SMEM((ngx, LANES), i32),
            pltpu.VMEM((tiles, nz, LANES), f32),
            trace, trace, trace, trace,
            pltpu.VMEM((2, nz + levels, LANES), f32),
            pltpu.VMEM((2, nz + levels, LANES), f32),
            pltpu.VMEM((2, columns, LANES), f32),
            pltpu.VMEM((2, columns, LANES), f32),
            pltpu.VMEM((ngy, nz, width), f32),
            dma((ngx,)), dma((ngx,)), dma((ngx,)), dma((ngx,)), dma((ngx,)), dma((ngx,)),
            dma((2,)), dma((2,)), dma((2,)), dma((2,)), dma((ngy,)), dma((ngy,)),
        ],
        compiler_params=pltpu.CompilerParams(
            collective_id=0, has_side_effects=True, vmem_limit_bytes=40 * 2**20
        ),
    )(
        fields.reshape(nz * columns, span),
        viscosity.reshape(levels * columns, span),
        precursor,
        tile_index.reshape(1, -1),
        g, gn, partner_gx, partner_col,
    )
    fine_out = halves_out(go.reshape(tiles, nfield, levels, 8, LANES))
    return fo.reshape(fields.shape), fine_out


def solution(mesh):
    return jax.shard_map(
        on_device,
        mesh=mesh,
        in_specs=(
            P(None, None, "gx", "gy"),
            P(None, "gx", "gy"),
            P(None, None, "gy"),
            P("gy"),
            P(("gx", "gy"), None, None, None, None),
            P(("gx", "gy"), None, None, None),
            P(("gx", "gy")),
            P(("gx", "gy")),
        ),
        out_specs=(P(None, None, "gx", "gy"), P(("gx", "gy"), None, None, None, None)),
        check_vma=False,
    )
```

```python
import functools

import jax
import jax.numpy as jnp
from jax import lax
from jax.experimental import pallas as pl
from jax.experimental.pallas import tpu as pltpu
from jax.sharding import PartitionSpec as P

CAP = 2
LANES = 128

time_step = 0.2
vertical_mix = 0.1
coarse_penalty = 0.5
fine_penalty = 1.0


def lane_take(rows, index):
    return jnp.take_along_axis(rows, index, axis=1, mode="promise_in_bounds")


def kernel(
    ngx, ngy, nfield, levels, columns, tiles, width,
    f_hbm, n_hbm, p_hbm, ti_hbm, g_hbm, gn_hbm, pgx_hbm, pcol_hbm,
    fo_ref, go_ref,
    f_ref, n_ref, p_ref, ti_ref, g_ref, gn_ref, pgx_ref, pcol_ref, in_sems,
    tid, col_send, col_recv, ctr, tr_send, tr_recv, an_send, an_recv,
    hx_send, hx_recv, hy_send, hy_recv, pr,
    col_ss, col_rs, tr_ss, tr_rs, an_ss, an_rs, hx_ss, hx_rs, hy_ss, hy_rs, pr_ss, pr_rs,
):
    mx, my = lax.axis_index("gx"), lax.axis_index("gy")
    nz = nfield * levels

    def x_peer(d):
        return (lax.rem(mx + d + ngx, ngx), my)

    def y_peer(d):
        return (mx, lax.rem(my + d + ngy, ngy))

    barrier = pltpu.get_barrier_semaphore()
    for d in range(1, ngx):
        pl.semaphore_signal(barrier, inc=1, device_id=x_peer(d), device_id_type=pl.DeviceIdType.MESH)
    for d in range(1, ngy):
        pl.semaphore_signal(barrier, inc=1, device_id=y_peer(d), device_id_type=pl.DeviceIdType.MESH)

    pgx_in, pcol_in, f_in, n_in, g_in, gn_in, p_in, ti_in = (
        pltpu.make_async_copy(src, dst, in_sems.at[i])
        for i, (src, dst) in enumerate(
            (
                (pgx_hbm, pgx_ref), (pcol_hbm, pcol_ref), (f_hbm, f_ref), (n_hbm, n_ref),
                (g_hbm, g_ref), (gn_hbm, gn_ref), (p_hbm, p_ref), (ti_hbm, ti_ref),
            )
        )
    )
    for c in (pgx_in, pcol_in, f_in, n_in, g_in, gn_in, p_in, ti_in):
        c.start()
    pgx_in.wait()
    pcol_in.wait()

    for d in range(ngx):
        goal = lax.rem(mx + d, ngx)
        first, last = jnp.int32(tiles), jnp.int32(-1)
        for t in range(tiles):
            hit = pgx_ref[t] == goal
            last = jnp.where(hit, t, last)
            u = tiles - 1 - t
            first = jnp.where(pgx_ref[u] == goal, u, first)
        for c, at in enumerate((first, last)):
            inside = jnp.clip(at, 0, tiles - 1)
            tid[d, c] = inside
            value = jnp.where(last < 0, -1, pcol_ref[inside])
            col_send[d, c] = value
            if d == 0:
                col_recv[d, c] = value

    pl.semaphore_wait(barrier, ngx + ngy - 2)

    def remote(src, dst, ss, rs, to):
        return pltpu.make_async_remote_copy(
            src_ref=src, dst_ref=dst, send_sem=ss, recv_sem=rs,
            device_id=to, device_id_type=pl.DeviceIdType.MESH,
        )

    col = [remote(col_send.at[d], col_recv.at[d], col_ss.at[d], col_rs.at[d], x_peer(d)) for d in range(1, ngx)]
    for c in col:
        c.start()

    rows = lax.broadcasted_iota(jnp.int32, (columns, LANES), 0)
    lanes = lax.broadcasted_iota(jnp.int32, (columns, LANES), 1)
    lane_z = lax.broadcasted_iota(jnp.int32, (nz, LANES), 1)

    def slab(k):
        return f_ref[k * columns : (k + 1) * columns, :]

    def nslab(z):
        return n_ref[z * columns : (z + 1) * columns, :]

    f_in.wait()
    n_in.wait()
    for side, row in ((0, columns - 1), (1, 0)):
        hx_send[side, 0:nz, :] = f_ref[pl.ds(row, nz, stride=columns), :]
        hx_send[side, nz : nz + levels, :] = n_ref[pl.ds(row, levels, stride=columns), :]
    for side, lane in ((0, LANES - 1), (1, 0)):
        packed = jnp.zeros((columns, LANES), jnp.float32)
        for k in range(nz + levels):
            s = slab(k) if k < nz else nslab(k - nz)
            packed = jnp.where(
                lanes == k, jnp.broadcast_to(s[:, lane : lane + 1], (columns, LANES)), packed
            )
        hy_send[side] = packed
    p_in.wait()
    for f in range(nfield):
        pr[0, f * levels : (f + 1) * levels, :] = p_ref[f]
    halo = [
        remote(hx_send.at[0], hx_recv.at[0], hx_ss.at[0], hx_rs.at[0], x_peer(1)),
        remote(hx_send.at[1], hx_recv.at[1], hx_ss.at[1], hx_rs.at[1], x_peer(-1)),
        remote(hy_send.at[0], hy_recv.at[0], hy_ss.at[0], hy_rs.at[0], y_peer(1)),
        remote(hy_send.at[1], hy_recv.at[1], hy_ss.at[1], hy_rs.at[1], y_peer(-1)),
    ]
    for c in halo:
        c.start()
    plane = [remote(pr.at[0], pr.at[d], pr_ss.at[d], pr_rs.at[d], y_peer(d)) for d in range(1, ngy)]

    @pl.when(mx == 0)
    def _():
        for c in plane:
            c.start()

    g_in.wait()
    even = (2 * lane_z) % LANES

    def coarsen(t, carry):
        g0 = g_ref[t, pl.ds(0, nz, stride=8), :]
        g1 = g_ref[t, pl.ds(4, nz, stride=8), :]
        r0, r1 = pltpu.roll(g0, 1, 1), pltpu.roll(g1, 1, 1)
        l0 = jnp.where(lane_z == 0, g0, r0)
        l1 = jnp.where(lane_z == 0, r0, r1)
        y0 = 0.5 * g0 + 0.25 * (l0 + pltpu.roll(g0, LANES - 1, 1))
        y1 = 0.5 * g1 + 0.25 * (l1 + pltpu.roll(g1, LANES - 1, 1))
        ctr[t] = jnp.where(lane_z < LANES // 2, lane_take(y0, even), lane_take(y1, even))
        return carry

    lax.fori_loop(0, tiles, coarsen, 0, unroll=8)
    traces = [remote(tr_send.at[d], tr_recv.at[d], tr_ss.at[d], tr_rs.at[d], x_peer(d)) for d in range(1, ngx)]
    for d in range(ngx):
        for c in range(CAP):
            if d == 0:
                tr_recv[0, c] = ctr[tid[0, c]]
            else:
                tr_send[d, c] = ctr[tid[d, c]]
        if d:
            traces[d - 1].start()

    answers = [remote(an_send.at[d], an_recv.at[d], an_ss.at[d], an_rs.at[d], x_peer(-d)) for d in range(1, ngx)]
    for d in range(ngx):
        if d:
            col[d - 1].wait_recv()
        for c in range(CAP):
            at = jnp.maximum(col_recv[d, c], 0)
            for k in range(nz):
                row = f_ref[pl.ds(k * columns + at, 1), :]
                if d:
                    an_send[d, c, k : k + 1, :] = row
                else:
                    an_recv[0, c, k : k + 1, :] = row
        if d:
            answers[d - 1].start()

    row8 = lax.broadcasted_iota(jnp.int32, (8, LANES), 0)
    lane8 = lax.broadcasted_iota(jnp.int32, (8, LANES), 1)
    x_last = (row8 % 4) == 3
    is_glue = (row8 % 4) == 0
    y_last = (lane8 == LANES - 1) & (row8 >= 4)
    lane_last, lane_first = lane8 == LANES - 1, lane8 == 0
    zero = jnp.zeros((8, LANES), jnp.float32)
    mix = time_step * vertical_mix
    own = [jnp.where(is_glue, 1.0 - time_step * fine_penalty, 1.0) - mix * m for m in range(3)]

    def up_x(q):
        return pltpu.roll(q, 7, 0)

    def down_x(q):
        return pltpu.roll(q, 1, 0)

    def up_y(q):
        r = pltpu.roll(q, LANES - 1, 1)
        return jnp.where(lane_last, pltpu.roll(r, 4, 0), r)

    def down_y(q):
        r = pltpu.roll(q, 1, 1)
        return jnp.where(lane_first, pltpu.roll(r, 4, 0), r)

    def fine(t, carry):
        for z in range(levels):
            n = gn_ref[t, z * 8 : z * 8 + 8, :]
            u = time_step * g_ref[t, z * 8 : z * 8 + 8, :]
            v = time_step * g_ref[t, (levels + z) * 8 : (levels + z) * 8 + 8, :]
            n = (2.0 * time_step) * n
            nx = n + up_x(n)
            ny = n + up_y(n)
            ae, aw = nx - u, down_x(nx) + u
            an, as_ = ny - v, down_y(ny) + v
            for f in range(nfield):
                k = f * levels + z
                q = g_ref[t, k * 8 : k * 8 + 8, :]
                e = jnp.where(x_last, zero, up_x(q) - q)
                w = down_x(e)
                nn = jnp.where(y_last, zero, up_y(q) - q)
                s = down_y(nn)
                near = [h for h in (k - 1, k + 1) if h // levels == f]
                beside = [g_ref[t, h * 8 : h * 8 + 8, :] for h in near]
                out = own[len(near)] * q + mix * sum(beside[1:], beside[0])
                out = out + ae * e - aw * w + an * nn - as_ * s
                go_ref[t, k * 8 : k * 8 + 8, :] = out
        return carry

    gn_in.wait()
    lax.fori_loop(0, tiles, fine, 0, unroll=2)

    ti_in.wait()
    for c in halo:
        c.wait_recv()

    @pl.when(mx == 0)
    def _():
        for c in plane:
            c.wait_recv()
        index = jnp.broadcast_to(ti_ref[...], (nz, LANES))
        per = LANES // width
        inflow = jnp.zeros((nz, LANES), jnp.float32)
        for b in range(ngy * width // LANES):
            parts = [pr[lax.rem(my - (b * per + i) + ngy, ngy)] for i in range(per)]
            block = parts[0] if per == 1 else jnp.concatenate(parts, axis=1)
            inflow = jnp.where(index // LANES == b, lane_take(block, index % LANES), inflow)
        hx_recv[0, 0:nz, :] = inflow
        hx_recv[0, nz : nz + levels, :] = n_ref[pl.ds(0, levels, stride=columns), :]

    @pl.when(mx == ngx - 1)
    def _():
        hx_recv[1, 0:nz, :] = f_ref[pl.ds(columns - 1, nz, stride=columns), :]
        hx_recv[1, nz : nz + levels, :] = n_ref[pl.ds(columns - 1, levels, stride=columns), :]

    for c in traces:
        c.wait_recv()
    count = jnp.zeros((columns, LANES), jnp.float32)
    for d in range(ngx):
        for c in range(CAP):
            count = count + jnp.where(rows == col_recv[d, c], 1.0, 0.0)
    keep = 1.0 - (time_step * coarse_penalty) * count

    def glue(f, carry):
        total = [jnp.zeros((columns, LANES), jnp.float32)] * levels
        for d in range(ngx):
            for c in range(CAP):
                here = rows == col_recv[d, c]
                for z in range(levels):
                    row = tr_recv[d, c, pl.ds(f * levels + z, 1), :]
                    total[z] = total[z] + jnp.where(here, jnp.broadcast_to(row, (columns, LANES)), 0.0)
        for z in range(levels):
            at = pl.multiple_of((f * levels + z) * columns, columns)
            fo_ref[pl.ds(at, columns), :] = (
                keep * f_ref[pl.ds(at, columns), :] + (time_step * coarse_penalty) * total[z]
            )
        return carry

    lax.fori_loop(0, nfield, glue, 0)

    def around(q, k):
        e = jnp.where(rows == columns - 1, hx_recv[1, k : k + 1, :], pltpu.roll(q, columns - 1, 0))
        w = jnp.where(rows == 0, hx_recv[0, k : k + 1, :], pltpu.roll(q, 1, 0))
        n = jnp.where(lanes == LANES - 1, hy_recv[1, :, k : k + 1], pltpu.roll(q, LANES - 1, 1))
        s = jnp.where(lanes == 0, hy_recv[0, :, k : k + 1], pltpu.roll(q, 1, 1))
        return e, w, n, s

    half = 0.5 * time_step
    for z in range(levels):
        n = nslab(z)
        ne, nw, nn, ns = around(n, nz + z)
        u, v = slab(z), slab(levels + z)
        ae, aw = half * (n + ne - u), half * (n + nw + u)
        an, as_ = half * (n + nn - v), half * (n + ns + v)
        for f in range(nfield):
            k = f * levels + z
            q = slab(k)
            e, w, north, south = around(q, k)
            out = ae * (e - q) - aw * (q - w) + an * (north - q) - as_ * (q - south)
            if z < levels - 1:
                out = out + (time_step * vertical_mix) * (slab(k + 1) - q)
            if z > 0:
                out = out - (time_step * vertical_mix) * (q - slab(k - 1))
            at = k * columns
            fo_ref[at : at + columns, :] = fo_ref[at : at + columns, :] + out

    for c in answers:
        c.wait_recv()
    low = lane_z // 2
    low_up = low + lane_z % 2
    high = low + LANES // 2
    high_up = jnp.minimum(low_up + LANES // 2, LANES - 1)

    def settle(t, carry):
        goal = pgx_ref[t]
        d = lax.rem(goal - mx + ngx, ngx)
        c = jnp.where(tid[d, 0] == t, 0, 1)
        a = (0.5 * time_step * fine_penalty) * an_recv[d, c]
        r0 = lane_take(a, low) + lane_take(a, low_up)
        r1 = lane_take(a, high) + lane_take(a, high_up)
        for k in range(nz):
            b0 = jnp.broadcast_to(r0[k : k + 1, :], (8, LANES))
            b1 = jnp.broadcast_to(r1[k : k + 1, :], (8, LANES))
            add = jnp.where(is_glue, jnp.where(row8 < 4, b0, b1), zero)
            go_ref[t, k * 8 : k * 8 + 8, :] = go_ref[t, k * 8 : k * 8 + 8, :] + add
        return carry

    lax.fori_loop(0, tiles, settle, 0, unroll=4)

    for c in col + halo + traces + answers:
        c.wait_send()

    @pl.when(mx == 0)
    def _():
        for c in plane:
            c.wait_send()


def halves_in(a):
    lead = a.shape[:-2]
    a = a.reshape(lead + (a.shape[-2], 2, LANES))
    a = jnp.swapaxes(a, -3, -2)
    return a.reshape(lead + (2 * a.shape[-2], LANES))


def halves_out(a):
    lead = a.shape[:-2]
    a = a.reshape(lead + (2, a.shape[-2] // 2, LANES))
    a = jnp.swapaxes(a, -3, -2)
    return a.reshape(lead + (a.shape[-3], 2 * LANES))


def on_device(
    fields, viscosity, precursor, tile_index, fine_fields, fine_viscosity, partner_gx, partner_col
):
    ngx, ngy = lax.axis_size("gx"), lax.axis_size("gy")
    nfield, levels, columns, span = fields.shape
    nz = nfield * levels
    tiles = fine_fields.shape[0]
    width = precursor.shape[2]
    f32, i32 = jnp.float32, jnp.int32
    g = halves_in(fine_fields).reshape(tiles, nz * 8, LANES)
    gn = halves_in(fine_viscosity).reshape(tiles, levels * 8, LANES)
    vmem = pl.BlockSpec(memory_space=pltpu.VMEM)
    dma = pltpu.SemaphoreType.DMA
    trace = pltpu.VMEM((ngx, CAP, nz, LANES), f32)
    fo, go = pl.pallas_call(
        functools.partial(kernel, ngx, ngy, nfield, levels, columns, tiles, width),
        out_shape=(
            jax.ShapeDtypeStruct((nz * columns, span), f32),
            jax.ShapeDtypeStruct((tiles, nz * 8, LANES), f32),
        ),
        in_specs=[pl.BlockSpec(memory_space=pltpu.HBM)] * 8,
        out_specs=(vmem, vmem),
        scratch_shapes=[
            pltpu.VMEM((nz * columns, span), f32),
            pltpu.VMEM((levels * columns, span), f32),
            pltpu.VMEM(precursor.shape, f32),
            pltpu.VMEM((1, tile_index.shape[0]), i32),
            pltpu.VMEM(g.shape, f32),
            pltpu.VMEM(gn.shape, f32),
            pltpu.SMEM(partner_gx.shape, i32),
            pltpu.SMEM(partner_col.shape, i32),
            dma((8,)),
            pltpu.SMEM((ngx, CAP), i32),
            pltpu.SMEM((ngx, LANES), i32),
            pltpu.SMEM((ngx, LANES), i32),
            pltpu.VMEM((tiles, nz, LANES), f32),
            trace, trace, trace, trace,
            pltpu.VMEM((2, nz + levels, LANES), f32),
            pltpu.VMEM((2, nz + levels, LANES), f32),
            pltpu.VMEM((2, columns, LANES), f32),
            pltpu.VMEM((2, columns, LANES), f32),
            pltpu.VMEM((ngy, nz, width), f32),
            dma((ngx,)), dma((ngx,)), dma((ngx,)), dma((ngx,)), dma((ngx,)), dma((ngx,)),
            dma((2,)), dma((2,)), dma((2,)), dma((2,)), dma((ngy,)), dma((ngy,)),
        ],
        compiler_params=pltpu.CompilerParams(
            collective_id=0, has_side_effects=True, vmem_limit_bytes=40 * 2**20
        ),
    )(*(pltpu.with_memory_space_constraint(a, pltpu.HBM) for a in (
        fields.reshape(nz * columns, span),
        viscosity.reshape(levels * columns, span),
        precursor,
        tile_index.reshape(1, -1),
        g, gn, partner_gx, partner_col,
    )))
    fine_out = halves_out(go.reshape(tiles, nfield, levels, 8, LANES))
    return fo.reshape(fields.shape), fine_out


def solution(mesh):
    return jax.shard_map(
        on_device,
        mesh=mesh,
        in_specs=(
            P(None, None, "gx", "gy"),
            P(None, "gx", "gy"),
            P(None, None, "gy"),
            P("gy"),
            P(("gx", "gy"), None, None, None, None),
            P(("gx", "gy"), None, None, None),
            P(("gx", "gy")),
            P(("gx", "gy")),
        ),
        out_specs=(P(None, None, "gx", "gy"), P(("gx", "gy"), None, None, None, None)),
        check_vma=False,
    )
```

```python
import functools

import jax
import jax.numpy as jnp
from jax import lax
from jax.experimental import pallas as pl
from jax.experimental.pallas import tpu as pltpu
from jax.sharding import PartitionSpec as P

CAP = 2
LANES = 128

time_step = 0.2
vertical_mix = 0.1
coarse_penalty = 0.5
fine_penalty = 1.0


def lane_take(rows, index):
    return jnp.take_along_axis(rows, index, axis=1, mode="promise_in_bounds")


def kernel(
    ngx, ngy, nfield, levels, columns, tiles, width,
    f_hbm, n_hbm, p_hbm, ti_hbm, g_hbm, gn_hbm, pgx_hbm, pcol_hbm,
    fo_ref, go_ref, at_ref,
    f_ref, n_ref, p_ref, ti_ref, g_ref, gn_ref, pgx_ref, pcol_ref, in_sems,
    tid, col_send, col_recv, ctr, tr_send, tr_recv, an_send, an_recv,
    hx_send, hx_recv, hy_send, hy_recv, pr,
    col_ss, col_rs, tr_ss, tr_rs, an_ss, an_rs, hx_ss, hx_rs, hy_ss, hy_rs, pr_ss, pr_rs,
):
    mx, my = lax.axis_index("gx"), lax.axis_index("gy")
    nz = nfield * levels

    def x_peer(d):
        return (lax.rem(mx + d + ngx, ngx), my)

    def y_peer(d):
        return (mx, lax.rem(my + d + ngy, ngy))

    barrier = pltpu.get_barrier_semaphore()
    for d in range(1, ngx):
        pl.semaphore_signal(barrier, inc=1, device_id=x_peer(d), device_id_type=pl.DeviceIdType.MESH)
    for d in range(1, ngy):
        pl.semaphore_signal(barrier, inc=1, device_id=y_peer(d), device_id_type=pl.DeviceIdType.MESH)

    pgx_in, pcol_in, f_in, n_in, g_in, gn_in, p_in, ti_in = (
        pltpu.make_async_copy(src, dst, in_sems.at[i])
        for i, (src, dst) in enumerate(
            (
                (pgx_hbm, pgx_ref), (pcol_hbm, pcol_ref), (f_hbm, f_ref), (n_hbm, n_ref),
                (g_hbm, g_ref), (gn_hbm, gn_ref), (p_hbm, p_ref), (ti_hbm, ti_ref),
            )
        )
    )
    for c in (pgx_in, pcol_in, f_in, n_in, g_in, gn_in, p_in, ti_in):
        c.start()
    pgx_in.wait()
    pcol_in.wait()

    for d in range(ngx):
        goal = lax.rem(mx + d, ngx)
        first, last = jnp.int32(tiles), jnp.int32(-1)
        for t in range(tiles):
            hit = pgx_ref[t] == goal
            last = jnp.where(hit, t, last)
            u = tiles - 1 - t
            first = jnp.where(pgx_ref[u] == goal, u, first)
        for c, at in enumerate((first, last)):
            inside = jnp.clip(at, 0, tiles - 1)
            tid[d, c] = inside
            value = jnp.where(last < 0, -1, pcol_ref[inside])
            col_send[d, c] = value
            if d == 0:
                col_recv[d, c] = value

    pl.semaphore_wait(barrier, ngx + ngy - 2)

    def remote(src, dst, ss, rs, to):
        return pltpu.make_async_remote_copy(
            src_ref=src, dst_ref=dst, send_sem=ss, recv_sem=rs,
            device_id=to, device_id_type=pl.DeviceIdType.MESH,
        )

    col = [remote(col_send.at[d], col_recv.at[d], col_ss.at[d], col_rs.at[d], x_peer(d)) for d in range(1, ngx)]
    for c in col:
        c.start()

    rows = lax.broadcasted_iota(jnp.int32, (columns, LANES), 0)
    lanes = lax.broadcasted_iota(jnp.int32, (columns, LANES), 1)
    lane_z = lax.broadcasted_iota(jnp.int32, (nz, LANES), 1)

    def slab(k):
        return f_ref[k * columns : (k + 1) * columns, :]

    def nslab(z):
        return n_ref[z * columns : (z + 1) * columns, :]

    f_in.wait()
    n_in.wait()
    for side, row in ((0, columns - 1), (1, 0)):
        hx_send[side, 0:nz, :] = f_ref[pl.ds(row, nz, stride=columns), :]
        hx_send[side, nz : nz + levels, :] = n_ref[pl.ds(row, levels, stride=columns), :]
    for side, lane in ((0, LANES - 1), (1, 0)):
        packed = jnp.zeros((columns, LANES), jnp.float32)
        for k in range(nz + levels):
            s = slab(k) if k < nz else nslab(k - nz)
            packed = jnp.where(
                lanes == k, jnp.broadcast_to(s[:, lane : lane + 1], (columns, LANES)), packed
            )
        hy_send[side] = packed
    p_in.wait()
    for f in range(nfield):
        pr[0, f * levels : (f + 1) * levels, :] = p_ref[f]
    halo = [
        remote(hx_send.at[0], hx_recv.at[0], hx_ss.at[0], hx_rs.at[0], x_peer(1)),
        remote(hx_send.at[1], hx_recv.at[1], hx_ss.at[1], hx_rs.at[1], x_peer(-1)),
        remote(hy_send.at[0], hy_recv.at[0], hy_ss.at[0], hy_rs.at[0], y_peer(1)),
        remote(hy_send.at[1], hy_recv.at[1], hy_ss.at[1], hy_rs.at[1], y_peer(-1)),
    ]
    for c in halo:
        c.start()
    plane = [remote(pr.at[0], pr.at[d], pr_ss.at[d], pr_rs.at[d], y_peer(d)) for d in range(1, ngy)]

    @pl.when(mx == 0)
    def _():
        for c in plane:
            c.start()

    g_in.wait()
    even = (2 * lane_z) % LANES

    def coarsen(t, carry):
        g0 = g_ref[t, pl.ds(0, nz, stride=8), :]
        g1 = g_ref[t, pl.ds(4, nz, stride=8), :]
        r0, r1 = pltpu.roll(g0, 1, 1), pltpu.roll(g1, 1, 1)
        l0 = jnp.where(lane_z == 0, g0, r0)
        l1 = jnp.where(lane_z == 0, r0, r1)
        y0 = 0.5 * g0 + 0.25 * (l0 + pltpu.roll(g0, LANES - 1, 1))
        y1 = 0.5 * g1 + 0.25 * (l1 + pltpu.roll(g1, LANES - 1, 1))
        ctr[t] = jnp.where(lane_z < LANES // 2, lane_take(y0, even), lane_take(y1, even))
        return carry

    lax.fori_loop(0, tiles, coarsen, 0, unroll=8)
    traces = [remote(tr_send.at[d], tr_recv.at[d], tr_ss.at[d], tr_rs.at[d], x_peer(d)) for d in range(1, ngx)]
    for d in range(ngx):
        for c in range(CAP):
            if d == 0:
                tr_recv[0, c] = ctr[tid[0, c]]
            else:
                tr_send[d, c] = ctr[tid[d, c]]
        if d:
            traces[d - 1].start()

    answers = [remote(an_send.at[d], an_recv.at[d], an_ss.at[d], an_rs.at[d], x_peer(-d)) for d in range(1, ngx)]
    for d in range(ngx):
        if d:
            col[d - 1].wait_recv()
        for c in range(CAP):
            at = jnp.maximum(col_recv[d, c], 0)
            found = f_ref[pl.ds(at, nz, stride=columns), :]
            if d:
                an_send[d, c] = found
            else:
                an_recv[0, c] = found
        if d:
            answers[d - 1].start()

    row8 = lax.broadcasted_iota(jnp.int32, (8, LANES), 0)
    lane8 = lax.broadcasted_iota(jnp.int32, (8, LANES), 1)
    x_last = (row8 % 4) == 3
    is_glue = (row8 % 4) == 0
    y_last = (lane8 == LANES - 1) & (row8 >= 4)
    lane_last, lane_first = lane8 == LANES - 1, lane8 == 0
    zero = jnp.zeros((8, LANES), jnp.float32)
    mix = time_step * vertical_mix
    own = [jnp.where(is_glue, 1.0 - time_step * fine_penalty, 1.0) - mix * m for m in range(3)]

    def up_x(q):
        return pltpu.roll(q, 7, 0)

    def down_x(q):
        return pltpu.roll(q, 1, 0)

    def up_y(q):
        r = pltpu.roll(q, LANES - 1, 1)
        return jnp.where(lane_last, pltpu.roll(r, 4, 0), r)

    def down_y(q):
        r = pltpu.roll(q, 1, 1)
        return jnp.where(lane_first, pltpu.roll(r, 4, 0), r)

    def fine(t, carry):
        for z in range(levels):
            n = gn_ref[t, z * 8 : z * 8 + 8, :]
            u = time_step * g_ref[t, z * 8 : z * 8 + 8, :]
            v = time_step * g_ref[t, (levels + z) * 8 : (levels + z) * 8 + 8, :]
            n = (2.0 * time_step) * n
            nx = n + up_x(n)
            ny = n + up_y(n)
            ae, aw = nx - u, down_x(nx) + u
            an, as_ = ny - v, down_y(ny) + v
            for f in range(nfield):
                k = f * levels + z
                q = g_ref[t, k * 8 : k * 8 + 8, :]
                e = jnp.where(x_last, zero, up_x(q) - q)
                w = down_x(e)
                nn = jnp.where(y_last, zero, up_y(q) - q)
                s = down_y(nn)
                near = [h for h in (k - 1, k + 1) if h // levels == f]
                beside = [g_ref[t, h * 8 : h * 8 + 8, :] for h in near]
                out = own[len(near)] * q + mix * sum(beside[1:], beside[0])
                out = out + ae * e - aw * w + an * nn - as_ * s
                go_ref[t, k * 8 : k * 8 + 8, :] = out
        return carry

    gn_in.wait()
    lax.fori_loop(0, tiles, fine, 0, unroll=2)

    ti_in.wait()
    for c in halo:
        c.wait_recv()

    @pl.when(mx == 0)
    def _():
        for c in plane:
            c.wait_recv()
        index = jnp.broadcast_to(ti_ref[...], (nz, LANES))
        per = LANES // width
        inflow = jnp.zeros((nz, LANES), jnp.float32)
        for b in range(ngy * width // LANES):
            parts = [pr[lax.rem(my - (b * per + i) + ngy, ngy)] for i in range(per)]
            block = parts[0] if per == 1 else jnp.concatenate(parts, axis=1)
            inflow = jnp.where(index // LANES == b, lane_take(block, index % LANES), inflow)
        hx_recv[0, 0:nz, :] = inflow
        hx_recv[0, nz : nz + levels, :] = n_ref[pl.ds(0, levels, stride=columns), :]

    @pl.when(mx == ngx - 1)
    def _():
        hx_recv[1, 0:nz, :] = f_ref[pl.ds(columns - 1, nz, stride=columns), :]
        hx_recv[1, nz : nz + levels, :] = n_ref[pl.ds(columns - 1, levels, stride=columns), :]

    for c in traces:
        c.wait_recv()
    count = jnp.zeros((columns, LANES), jnp.float32)
    for d in range(ngx):
        for c in range(CAP):
            count = count + jnp.where(rows == col_recv[d, c], 1.0, 0.0)
    keep = 1.0 - (time_step * coarse_penalty) * count

    def glue(f, carry):
        total = [jnp.zeros((columns, LANES), jnp.float32)] * levels
        for d in range(ngx):
            for c in range(CAP):
                here = rows == col_recv[d, c]
                for z in range(levels):
                    row = tr_recv[d, c, pl.ds(f * levels + z, 1), :]
                    total[z] = total[z] + jnp.where(here, jnp.broadcast_to(row, (columns, LANES)), 0.0)
        for z in range(levels):
            at = pl.multiple_of((f * levels + z) * columns, columns)
            fo_ref[pl.ds(at, columns), :] = (
                keep * f_ref[pl.ds(at, columns), :] + (time_step * coarse_penalty) * total[z]
            )
        return carry

    lax.fori_loop(0, nfield, glue, 0)

    def around(q, k):
        e = jnp.where(rows == columns - 1, hx_recv[1, k : k + 1, :], pltpu.roll(q, columns - 1, 0))
        w = jnp.where(rows == 0, hx_recv[0, k : k + 1, :], pltpu.roll(q, 1, 0))
        n = jnp.where(lanes == LANES - 1, hy_recv[1, :, k : k + 1], pltpu.roll(q, LANES - 1, 1))
        s = jnp.where(lanes == 0, hy_recv[0, :, k : k + 1], pltpu.roll(q, 1, 1))
        return e, w, n, s

    half = 0.5 * time_step
    for z in range(levels):
        n = nslab(z)
        ne, nw, nn, ns = around(n, nz + z)
        u, v = slab(z), slab(levels + z)
        ae, aw = half * (n + ne - u), half * (n + nw + u)
        an, as_ = half * (n + nn - v), half * (n + ns + v)
        for f in range(nfield):
            k = f * levels + z
            q = slab(k)
            e, w, north, south = around(q, k)
            out = ae * (e - q) - aw * (q - w) + an * (north - q) - as_ * (q - south)
            if z < levels - 1:
                out = out + (time_step * vertical_mix) * (slab(k + 1) - q)
            if z > 0:
                out = out - (time_step * vertical_mix) * (q - slab(k - 1))
            at = k * columns
            fo_ref[at : at + columns, :] = fo_ref[at : at + columns, :] + out

    for c in answers:
        c.wait_recv()
    for t in range(tiles):
        d = lax.rem(pgx_ref[t] - mx + ngx, ngx)
        at_ref[t] = an_recv[d, jnp.where(tid[d, 0] == t, 0, 1)]

    for c in col + halo + traces + answers:
        c.wait_send()

    @pl.when(mx == 0)
    def _():
        for c in plane:
            c.wait_send()


def settle_kernel(nz, chunk, fo_ref, go_ref, at_ref, fo_hbm, go_hbm, done, sems):
    tiles = go_ref.shape[0]
    outer = pltpu.make_async_copy(fo_ref, fo_hbm, sems.at[tiles // chunk])
    outer.start()
    lane_z = lax.broadcasted_iota(jnp.int32, (nz, LANES), 1)
    row8 = lax.broadcasted_iota(jnp.int32, (8, LANES), 0)
    is_glue, first_half = (row8 % 4) == 0, row8 < 4
    low = lane_z // 2
    low_up = low + lane_z % 2
    high = low + LANES // 2
    high_up = jnp.minimum(low_up + LANES // 2, LANES - 1)
    copies = []
    for j in range(tiles // chunk):
        for t in range(j * chunk, (j + 1) * chunk):
            a = (0.5 * time_step * fine_penalty) * at_ref[t]
            r0 = lane_take(a, low) + lane_take(a, low_up)
            r1 = lane_take(a, high) + lane_take(a, high_up)
            for k in range(nz):
                b0 = jnp.broadcast_to(r0[k : k + 1, :], (8, LANES))
                b1 = jnp.broadcast_to(r1[k : k + 1, :], (8, LANES))
                add = jnp.where(is_glue, jnp.where(first_half, b0, b1), 0.0)
                done[t, k * 8 : k * 8 + 8, :] = go_ref[t, k * 8 : k * 8 + 8, :] + add
        part = pl.ds(j * chunk, chunk)
        copies.append(pltpu.make_async_copy(done.at[part], go_hbm.at[part], sems.at[j]))
        copies[-1].start()
    for c in copies:
        c.wait()
    outer.wait()


def halves_in(a):
    lead = a.shape[:-2]
    a = a.reshape(lead + (a.shape[-2], 2, LANES))
    a = jnp.swapaxes(a, -3, -2)
    return a.reshape(lead + (2 * a.shape[-2], LANES))


def halves_out(a):
    lead = a.shape[:-2]
    a = a.reshape(lead + (2, a.shape[-2] // 2, LANES))
    a = jnp.swapaxes(a, -3, -2)
    return a.reshape(lead + (a.shape[-3], 2 * LANES))


def on_device(
    fields, viscosity, precursor, tile_index, fine_fields, fine_viscosity, partner_gx, partner_col
):
    ngx, ngy = lax.axis_size("gx"), lax.axis_size("gy")
    nfield, levels, columns, span = fields.shape
    nz = nfield * levels
    tiles = fine_fields.shape[0]
    width = precursor.shape[2]
    f32, i32 = jnp.float32, jnp.int32
    g = halves_in(fine_fields).reshape(tiles, nz * 8, LANES)
    gn = halves_in(fine_viscosity).reshape(tiles, levels * 8, LANES)
    vmem = pl.BlockSpec(memory_space=pltpu.VMEM)
    dma = pltpu.SemaphoreType.DMA
    trace = pltpu.VMEM((ngx, CAP, nz, LANES), f32)
    fo, go, answer = pl.pallas_call(
        functools.partial(kernel, ngx, ngy, nfield, levels, columns, tiles, width),
        out_shape=(
            jax.ShapeDtypeStruct((nz * columns, span), f32),
            jax.ShapeDtypeStruct((tiles, nz * 8, LANES), f32),
            jax.ShapeDtypeStruct((tiles, nz, LANES), f32),
        ),
        in_specs=[pl.BlockSpec(memory_space=pltpu.HBM)] * 8,
        out_specs=(vmem, vmem, vmem),
        scratch_shapes=[
            pltpu.VMEM((nz * columns, span), f32),
            pltpu.VMEM((levels * columns, span), f32),
            pltpu.VMEM(precursor.shape, f32),
            pltpu.VMEM((1, tile_index.shape[0]), i32),
            pltpu.VMEM(g.shape, f32),
            pltpu.VMEM(gn.shape, f32),
            pltpu.SMEM(partner_gx.shape, i32),
            pltpu.SMEM(partner_col.shape, i32),
            dma((8,)),
            pltpu.SMEM((ngx, CAP), i32),
            pltpu.SMEM((ngx, LANES), i32),
            pltpu.SMEM((ngx, LANES), i32),
            pltpu.VMEM((tiles, nz, LANES), f32),
            trace, trace, trace, trace,
            pltpu.VMEM((2, nz + levels, LANES), f32),
            pltpu.VMEM((2, nz + levels, LANES), f32),
            pltpu.VMEM((2, columns, LANES), f32),
            pltpu.VMEM((2, columns, LANES), f32),
            pltpu.VMEM((ngy, nz, width), f32),
            dma((ngx,)), dma((ngx,)), dma((ngx,)), dma((ngx,)), dma((ngx,)), dma((ngx,)),
            dma((2,)), dma((2,)), dma((2,)), dma((2,)), dma((ngy,)), dma((ngy,)),
        ],
        compiler_params=pltpu.CompilerParams(
            collective_id=0, has_side_effects=True, vmem_limit_bytes=40 * 2**20
        ),
    )(*(pltpu.with_memory_space_constraint(a, pltpu.HBM) for a in (
        fields.reshape(nz * columns, span),
        viscosity.reshape(levels * columns, span),
        precursor,
        tile_index.reshape(1, -1),
        g, gn, partner_gx, partner_col,
    )))
    chunk = 4
    hbm = pl.BlockSpec(memory_space=pltpu.HBM)
    fo, go = pl.pallas_call(
        functools.partial(settle_kernel, nz, chunk),
        out_shape=(pltpu.HBM(fo.shape, f32), pltpu.HBM(go.shape, f32)),
        in_specs=[vmem] * 3,
        out_specs=(hbm, hbm),
        scratch_shapes=[pltpu.VMEM(go.shape, f32), dma((tiles // chunk + 1,))],
        compiler_params=pltpu.CompilerParams(vmem_limit_bytes=20 * 2**20),
    )(fo, go, answer)
    fine_out = halves_out(go.reshape(tiles, nfield, levels, 8, LANES))
    return fo.reshape(fields.shape), fine_out


def solution(mesh):
    return jax.shard_map(
        on_device,
        mesh=mesh,
        in_specs=(
            P(None, None, "gx", "gy"),
            P(None, "gx", "gy"),
            P(None, None, "gy"),
            P("gy"),
            P(("gx", "gy"), None, None, None, None),
            P(("gx", "gy"), None, None, None),
            P(("gx", "gy")),
            P(("gx", "gy")),
        ),
        out_specs=(P(None, None, "gx", "gy"), P(("gx", "gy"), None, None, None, None)),
        check_vma=False,
    )
```
